32 devices in a mesh: problem: 2 (over y), worker: 4 (over z), head: 4 (over x, core).
Axes of the slice: x: 2, y: 2, z: 4, core: 2. Of those that a mesh axis runs over, the one named last changes fastest.
Arguments:
- queries: bfloat16 [8, 4, 40, 128], P(('problem', 'worker'), None, 'head'), parts along dimension 0, may hold values from -60 to 60
- cache_keys: bfloat16 [8, 2048, 8, 128], P(('problem', 'worker'), None, 'head'), parts along dimension 0, may hold values from -6 to 6
- cache_values: bfloat16 [8, 2048, 8, 128], P(('problem', 'worker'), None, 'head'), parts along dimension 0, may hold values from -6 to 6
- new_keys: bfloat16 [8, 4, 8, 128], P(('problem', 'worker'), None, 'head'), parts along dimension 0, may hold values from -6 to 6
- new_values: bfloat16 [8, 4, 8, 128], P(('problem', 'worker'), None, 'head'), parts along dimension 0, may hold values from -6 to 6
- lengths: int32 [8, 4], P(('problem', 'worker')), parts along dimension 0, may hold values from 1 to 2048, as said below
Outputs:
- attended: bfloat16 [8, 4, 40, 128], P(('problem', 'worker'), None, 'head'), parts along dimension 0
The draws below stay inside these ranges and needn't reach their ends.
There are 2 independent parts, one for each index of `problem`. The reference program is written for one: setup_inputs(seed, part) draws one part's arguments, and reference() takes and returns one part's arrays. A program takes and returns all parts, laid end to end along the dimension named above; each array names one. Nothing has to cross between parts.
Inputs may be any that keep to these rules, and one draw needn't show every extreme that they name: lengths never fall from one step to the next; some worker's length at the last step is exactly 2048.
All inputs are finite; a program needn't handle non-finite values.
Results may differ from the reference program's by a relative error of at most 0.005.
Values may be sent and summed in bfloat16 or wider, within the bound.
No kernel may reach another device: no remote copies, remote signals or barrier semaphores. Data moves between devices by JAX's collectives and lax.ppermute only.
A program may use at most 64 MiB of HBM per device.

```python
import jax
import jax.numpy as jnp
from jax import lax

Q_HEADS = 40
KV_HEADS = 8
HEAD_DIM = 128
GROUP_SIZE = 5
CACHE_LEN = 2048
DECODE_STEPS = 4
WORKERS = 4


def draw_queries(key, part):
    full_shape = (WORKERS, DECODE_STEPS, Q_HEADS, HEAD_DIM)
    result = jnp.clip(3.0 * jax.random.normal(jax.random.fold_in(key, 1), full_shape, jnp.float32), -18.0, 18.0)
    return result.astype(jnp.bfloat16)


def draw_cache_keys(key, part):
    full_shape = (WORKERS, CACHE_LEN, KV_HEADS, HEAD_DIM)
    result = jnp.clip(jax.random.normal(jax.random.fold_in(key, 2), full_shape, jnp.float32), -6.0, 6.0)
    return result.astype(jnp.bfloat16)


def draw_lengths(key, part):
    base_key = jax.random.fold_in(key, 3)
    shift_key, trim_key, growth_key, longest_key = jax.random.split(base_key, 4)
    halving_count = jax.random.randint(shift_key, (WORKERS,), 0, 4, jnp.int32)
    upper_bound = jnp.right_shift(jnp.full((WORKERS,), CACHE_LEN, jnp.int32), halving_count)
    trimmed = jax.random.randint(trim_key, (WORKERS,), 0, CACHE_LEN // 16 + 1, jnp.int32)
    starting = upper_bound - trimmed
    longest = jax.random.randint(longest_key, (), 0, WORKERS, jnp.int32)
    worker_ids = jnp.arange(WORKERS, dtype=jnp.int32)
    starting = jnp.where(worker_ids == longest, CACHE_LEN, starting)
    growth = jax.random.randint(growth_key, (WORKERS,), 0, 4, jnp.int32)
    step_ids = jnp.arange(DECODE_STEPS, dtype=jnp.int32)
    result = starting[:, None] - (DECODE_STEPS - 1 - step_ids)[None, :] * growth[:, None]
    return jnp.maximum(result, 1).astype(jnp.int32)


def steps_of(rng, extent, cuts, least, largest):
    factor_of, own = 1.0, jax.random.fold_in(rng, 6)
    for dim, shards_of in cuts:
        heights = jnp.exp(jax.random.uniform(jax.random.fold_in(own, dim), (shards_of,), jnp.float32, least / len(cuts), largest / len(cuts)))
        factor_of = factor_of * jnp.repeat(heights, extent[dim] // shards_of).reshape([-1 if axis == dim else 1 for axis in range(len(extent))])
    return factor_of


def bell_draw(own_key, dims, scale, limit, cuts=(), held_as=jnp.bfloat16):
    values = scale * jax.random.normal(own_key, dims, jnp.float32)
    if cuts:
        values = values * steps_of(own_key, dims, cuts, -0.22, 0.18)
    return jnp.clip(values, -limit, limit).astype(held_as)


def setup_inputs(seed: int = 0, part: int = 0) -> dict:
    keys = jax.random.split(jax.random.key(seed), 7)
    own_keys = jax.random.split(jax.random.fold_in(keys[6], part), 7)
    queries = draw_queries(jax.random.fold_in(jax.random.fold_in(keys[6], part), 71), part)
    cache_keys = draw_cache_keys(jax.random.fold_in(jax.random.fold_in(keys[6], part), 71), part)
    cache_values = bell_draw(own_keys[2], (WORKERS, CACHE_LEN, KV_HEADS, HEAD_DIM), 1.0, 6.0, ((0, 4), (2, 4)))
    new_keys = bell_draw(own_keys[3], (WORKERS, DECODE_STEPS, KV_HEADS, HEAD_DIM), 1.0, 6.0, ((0, 4), (2, 4)))
    new_values = bell_draw(own_keys[4], (WORKERS, DECODE_STEPS, KV_HEADS, HEAD_DIM), 1.0, 6.0, ((0, 4), (2, 4)))
    lengths = draw_lengths(jax.random.fold_in(jax.random.fold_in(keys[6], part), 71), part)
    return dict(queries=queries, cache_keys=cache_keys, cache_values=cache_values, new_keys=new_keys, new_values=new_values, lengths=lengths)


masked_score = -1.0e30


def fold_block(running, scores, visible, value_rows):
    maxima, totals, outputs = running
    fresh_max = jnp.maximum(maxima, jnp.max(jnp.where(visible, scores, masked_score), axis=-1))
    carried = jnp.exp(maxima - fresh_max)
    weights = jnp.where(visible, jnp.exp(scores - fresh_max[..., None]), 0.0)
    totals = totals * carried + jnp.sum(weights, axis=-1)
    rounded = weights.astype(jnp.bfloat16).astype(jnp.float32)
    outputs = outputs * carried[..., None] + jnp.einsum("krc,ckd->krd", rounded, value_rows.astype(jnp.float32))
    return fresh_max, totals, outputs


def reference(queries, cache_keys, cache_values, new_keys, new_values, lengths):
    score_scale = 1.0 / (HEAD_DIM ** 0.5)
    row_count = WORKERS * DECODE_STEPS * GROUP_SIZE
    query_rows = queries.astype(jnp.float32).reshape(WORKERS, DECODE_STEPS, KV_HEADS, GROUP_SIZE, HEAD_DIM)
    query_rows = query_rows.transpose(2, 0, 1, 3, 4).reshape(KV_HEADS, row_count, HEAD_DIM)
    row_index = jnp.arange(row_count, dtype=jnp.int32)
    row_worker = row_index // (DECODE_STEPS * GROUP_SIZE)
    row_step = (row_index // GROUP_SIZE) % DECODE_STEPS
    fresh_keys = new_keys.reshape(WORKERS * DECODE_STEPS, KV_HEADS, HEAD_DIM)
    fresh_values = new_values.reshape(WORKERS * DECODE_STEPS, KV_HEADS, HEAD_DIM)
    column_index = jnp.arange(WORKERS * DECODE_STEPS, dtype=jnp.int32)
    column_worker = column_index // DECODE_STEPS
    column_step = column_index % DECODE_STEPS
    visible = (column_step[None, :] < row_step[:, None]) | ((column_step[None, :] == row_step[:, None]) & (column_worker[None, :] == row_worker[:, None]))
    running = (jnp.full((KV_HEADS, row_count), masked_score, jnp.float32), jnp.zeros((KV_HEADS, row_count), jnp.float32), jnp.zeros((KV_HEADS, row_count, HEAD_DIM), jnp.float32))
    scores = jnp.einsum("krd,ckd->krc", query_rows, fresh_keys.astype(jnp.float32)) * score_scale
    running = fold_block(running, scores, visible[None], fresh_values)
    slot_index = jnp.arange(CACHE_LEN, dtype=jnp.int32)

    def absorb(running, worker_item):
        worker_keys, worker_values, worker_lengths = worker_item
        visible_len = worker_lengths[row_step]
        cache_visible = slot_index[None, :] < visible_len[:, None]
        cache_scores = jnp.einsum("krd,ckd->krc", query_rows, worker_keys.astype(jnp.float32)) * score_scale
        return fold_block(running, cache_scores, cache_visible[None], worker_values), None

    running, _ = lax.scan(absorb, running, (cache_keys, cache_values, lengths))
    maxima, totals, outputs = running
    combined = outputs / totals[..., None]
    combined = combined.reshape(KV_HEADS, WORKERS, DECODE_STEPS, GROUP_SIZE, HEAD_DIM).transpose(1, 2, 0, 3, 4)
    return combined.reshape(WORKERS, DECODE_STEPS, Q_HEADS, HEAD_DIM).astype(jnp.bfloat16)
```

```python
import functools
import math

import jax
import jax.numpy as jnp
from jax import lax
from jax.experimental import pallas as pl
from jax.experimental.pallas import tpu as pltpu
from jax.sharding import PartitionSpec as P

masked_score = -1e30
lane_width = 128
stat_rows = 8


def split_heads(source_ref, wide_ref, target_ref, kv_local):
    slots, width = target_ref.shape[0], source_ref.shape[1]
    wide_ref[...] = source_ref[...].astype(jnp.float32)
    for head in range(kv_local):
        picked = wide_ref[pl.ds(head, slots, stride=kv_local), :]
        target_ref[:, pl.ds(head * width, width)] = picked.astype(jnp.bfloat16)


def place_fresh(source_ref, small_ref, pad_ref, target_ref, kv_local):
    steps = source_ref.shape[0] // kv_local
    width = source_ref.shape[1]
    begin = target_ref.shape[0] - lane_width
    small_ref[...] = source_ref[...].astype(jnp.float32)
    pad_ref[...] = jnp.zeros_like(pad_ref)
    for head in range(kv_local):
        pad_ref[pl.ds(0, steps), pl.ds(head * width, width)] = small_ref[pl.ds(head, steps, stride=kv_local), :]
    target_ref[pl.ds(begin, lane_width), :] = pad_ref[...].astype(jnp.bfloat16)


def attend_block(query_rows, lengths_ref, keys_ref, values_ref, kv_local, steps, own):
    count, (per_worker, width) = len(query_rows), query_rows[0].shape
    rows = count * per_worker
    slots = keys_ref.shape[0] - lane_width
    row = lax.broadcasted_iota(jnp.int32, (rows, 1), 0)
    step = row % steps
    head = row % per_worker // (per_worker // kv_local)
    wide = jnp.concatenate([shard.astype(jnp.float32) for shard in query_rows], axis=0)
    queries = jnp.concatenate(
        [jnp.where(head == k, wide, 0.0) for k in range(kv_local)], axis=1
    ).astype(jnp.bfloat16)
    scale = width ** (-0.5) * math.log2(math.e)
    scores = (
        lax.dot_general(
            queries, keys_ref[...], (((1,), (1,)), ((), ())), preferred_element_type=jnp.float32
        )
        * scale
    )
    limit = jnp.zeros((rows, 1), jnp.int32)
    for t in range(steps):
        limit = jnp.where(step == t, lengths_ref[0, t], limit)
    column = lax.broadcasted_iota(jnp.int32, (rows, slots), 1)
    cached = jnp.where(column < limit, scores[:, :slots], masked_score)
    fresh_limit = step + 1 if own else step
    fresh_column = lax.broadcasted_iota(jnp.int32, (rows, lane_width), 1)
    fresh = jnp.where(fresh_column < fresh_limit, scores[:, slots:], masked_score)
    top = jnp.maximum(
        jnp.max(cached, axis=1, keepdims=True), jnp.max(fresh, axis=1, keepdims=True)
    )
    top = top.astype(jnp.bfloat16).astype(jnp.float32)
    cached_weights = jnp.exp2(cached - top)
    fresh_weights = jnp.exp2(fresh - top)
    total = jnp.sum(cached_weights, axis=1, keepdims=True) + jnp.sum(
        fresh_weights, axis=1, keepdims=True
    )
    weights = jnp.concatenate(
        [cached_weights.astype(jnp.bfloat16), fresh_weights.astype(jnp.bfloat16)], axis=1
    )
    both = jnp.dot(weights, values_ref[...], preferred_element_type=jnp.float32)
    outputs = both[:, :width]
    for k in range(1, kv_local):
        outputs = jnp.where(head == k, both[:, k * width : (k + 1) * width], outputs)
    return outputs, top, total


def to_lanes(column):
    rows = column.shape[0]
    shape = (rows, lane_width)
    here = lax.broadcasted_iota(jnp.int32, shape, 0) == lax.broadcasted_iota(jnp.int32, shape, 1)
    return jnp.sum(jnp.where(here, column, 0.0), axis=0, keepdims=True)


def to_column(line, rows):
    shape = (rows, lane_width)
    here = lax.broadcasted_iota(jnp.int32, shape, 0) == lax.broadcasted_iota(jnp.int32, shape, 1)
    return jnp.sum(jnp.where(here, line, 0.0), axis=1, keepdims=True)


def pack(outputs, top, total):
    high = total.astype(jnp.bfloat16).astype(jnp.float32)
    top_line, high_line, low_line = to_lanes(top), to_lanes(high), to_lanes(total - high)
    line = lax.broadcasted_iota(jnp.int32, (stat_rows, lane_width), 0)
    stats = jnp.where(line == 0, top_line, jnp.where(line == 1, high_line, low_line))
    return jnp.concatenate([outputs, stats], axis=0).astype(jnp.bfloat16)


def first_kernel(
    kv_local, steps, chunks, lengths_ref, query_hbm, cache_keys_hbm, cache_values_hbm, new_keys_hbm,
    new_values_hbm, keys_ref, values_ref, outputs_ref, stats_ref, query_ref, raw_keys_ref, raw_values_ref,
    new_ref, wide_ref, small_ref, pad_ref, cache_sem, small_sem,
):
    size = raw_keys_ref.shape[0] // chunks
    fetch = [
        [
            pltpu.make_async_copy(
                source.at[pl.ds(i * size, size)], target.at[pl.ds(i * size, size)], cache_sem.at[side, i]
            )
            for i in range(chunks)
        ]
        for side, (source, target) in enumerate(
            ((cache_keys_hbm, raw_keys_ref), (cache_values_hbm, raw_values_ref))
        )
    ]
    small = [
        pltpu.make_async_copy(query_hbm, query_ref, small_sem.at[0]),
        pltpu.make_async_copy(new_keys_hbm, new_ref.at[0], small_sem.at[1]),
        pltpu.make_async_copy(new_values_hbm, new_ref.at[1], small_sem.at[2]),
    ]
    for copy in small + fetch[0] + fetch[1]:
        copy.start()
    for copy in small:
        copy.wait()
    place_fresh(new_ref.at[0], small_ref.at[0], pad_ref.at[0], keys_ref, kv_local)
    place_fresh(new_ref.at[1], small_ref.at[1], pad_ref.at[1], values_ref, kv_local)
    for side, (raw_ref, target_ref) in enumerate(((raw_keys_ref, keys_ref), (raw_values_ref, values_ref))):
        for i in range(chunks):
            fetch[side][i].wait()
            part = pl.ds(i * size, size)
            split_heads(
                raw_ref.at[part], wide_ref.at[side, part], target_ref.at[pl.ds(i * size // kv_local, size // kv_local)], kv_local
            )
    outputs, top, total = attend_block(
        [query_ref[...]], lengths_ref, keys_ref, values_ref, kv_local, steps, True
    )
    outputs_ref[...] = outputs
    lane = lax.broadcasted_iota(jnp.int32, stats_ref.shape, 1)
    stats_ref[...] = jnp.where(lane == 0, top, total)


def other_kernel(kv_local, steps, count, lengths_ref, *refs):
    queries, (keys_ref, values_ref), packets = refs[:count], refs[count : count + 2], refs[count + 2 :]
    rows = queries[0].shape[0]
    results = attend_block(
        [query_ref[...] for query_ref in queries], lengths_ref, keys_ref, values_ref, kv_local, steps, False
    )
    for place, packet_ref in enumerate(packets):
        packet_ref[...] = pack(*[part[place * rows : (place + 1) * rows] for part in results])


def merge_kernel(rows, outputs_ref, stats_ref, *refs):
    packets, merged_ref = refs[:-1], refs[-1]
    stats = stats_ref[...]
    parts = [(outputs_ref[...], stats[:, 0:1], stats[:, 1:2])]
    for packet_ref in packets:
        packet = packet_ref[...].astype(jnp.float32)
        lines = packet[rows : rows + stat_rows]
        parts.append(
            (
                packet[:rows],
                to_column(lines[0:1], rows),
                to_column(lines[1:2] + lines[2:3], rows),
            )
        )
    highest = functools.reduce(jnp.maximum, [top for _, top, _ in parts])
    factors = [jnp.exp2(top - highest) for _, top, _ in parts]
    total = sum(factor * part[2] for factor, part in zip(factors, parts))
    merged = sum(factor * part[0] for factor, part in zip(factors, parts))
    merged_ref[...] = (merged / total).astype(merged_ref.dtype)


vmem = pl.BlockSpec(memory_space=pltpu.VMEM)
hbm = pl.BlockSpec(memory_space=pltpu.HBM)
smem = pl.BlockSpec(memory_space=pltpu.SMEM)
grant = 40 * 1024 * 1024


def shift(shard, offset, workers):
    return lax.ppermute(shard, "worker", [(i, (i + offset) % workers) for i in range(workers)])


def local(queries, cache_keys, cache_values, new_keys, new_values, lengths):
    _, steps, heads, width = queries.shape
    slots, kv_local = cache_keys.shape[1:3]
    rows = steps * heads
    workers = lax.axis_size("worker")
    chunks = max(1, slots // 512)
    flat = lambda cache: cache.reshape(-1, width)
    as_rows = lambda q: q[0].transpose(1, 0, 2).reshape(rows, width)
    prepared = jax.ShapeDtypeStruct((slots + lane_width, kv_local * width), jnp.bfloat16)
    packet = jax.ShapeDtypeStruct((rows + stat_rows, width), jnp.bfloat16)

    def first(query_rows):
        return pl.pallas_call(
            functools.partial(first_kernel, kv_local, steps, chunks),
            out_shape=(
                prepared,
                prepared,
                jax.ShapeDtypeStruct((rows, width), jnp.float32),
                jax.ShapeDtypeStruct((rows, lane_width), jnp.float32),
            ),
            in_specs=[smem] + [hbm] * 5,
            out_specs=(vmem,) * 4,
            scratch_shapes=[
                pltpu.VMEM((rows, width), jnp.bfloat16),
                pltpu.VMEM((slots * kv_local, width), jnp.bfloat16),
                pltpu.VMEM((slots * kv_local, width), jnp.bfloat16),
                pltpu.VMEM((2, steps * kv_local, width), jnp.bfloat16),
                pltpu.VMEM((2, slots * kv_local, width), jnp.float32),
                pltpu.VMEM((2, steps * kv_local, width), jnp.float32),
                pltpu.VMEM((2, lane_width, kv_local * width), jnp.float32),
                pltpu.SemaphoreType.DMA((2, chunks)),
                pltpu.SemaphoreType.DMA((3,)),
            ],
            compiler_params=pltpu.CompilerParams(vmem_limit_bytes=grant),
            name="own_rows",
        )(lengths, query_rows, flat(cache_keys), flat(cache_values), flat(new_keys), flat(new_values))

    def others(query_list, keys, values):
        count = len(query_list)
        return pl.pallas_call(
            functools.partial(other_kernel, kv_local, steps, count),
            out_shape=(packet,) * count,
            in_specs=[smem] + [vmem] * (count + 2),
            out_specs=(vmem,) * count,
            compiler_params=pltpu.CompilerParams(vmem_limit_bytes=grant),
            name="partner_rows",
        )(lengths, *query_list, keys, values)

    def merge(outputs, stats, packets):
        return pl.pallas_call(
            functools.partial(merge_kernel, rows),
            out_shape=jax.ShapeDtypeStruct((rows, width), jnp.bfloat16),
            in_specs=[vmem] * (2 + len(packets)),
            out_specs=vmem,
            compiler_params=pltpu.CompilerParams(vmem_limit_bytes=grant // 10),
            name="merge",
        )(outputs, stats, *packets)

    arrived = [as_rows(shift(queries, offset, workers)) for offset in range(1, workers)]
    keys, values, outputs, stats = first(as_rows(queries))
    sent = others(arrived, keys, values) if arrived else ()
    packets = [shift(p, -offset, workers) for offset, p in enumerate(sent, 1)]
    merged = merge(outputs, stats, packets)
    return merged.reshape(heads, steps, width).transpose(1, 0, 2)[None]


def solution(mesh):
    split = P(("problem", "worker"), None, "head", None)
    return jax.shard_map(
        local,
        mesh=mesh,
        in_specs=(split,) * 5 + (P(("problem", "worker"), None),),
        out_specs=split,
        check_vma=False,
    )
```

```python
import functools
import math

import jax
import jax.numpy as jnp
from jax import lax
from jax.experimental import pallas as pl
from jax.experimental.pallas import tpu as pltpu
from jax.sharding import PartitionSpec as P

masked_score = -1e30
lane_width = 128
stat_rows = 8


def pick_head(source_ref, wide_ref, kv_local):
    slots = source_ref.shape[0] // kv_local
    wide_ref[...] = source_ref[...].astype(jnp.float32)
    return [wide_ref[pl.ds(head, slots, stride=kv_local), :] for head in range(kv_local)]


def pad_fresh(source_ref, wide_ref, pad_ref, kv_local):
    parts = pick_head(source_ref, wide_ref, kv_local)
    steps, width = parts[0].shape
    pad_ref[...] = jnp.zeros_like(pad_ref)
    for head, part in enumerate(parts):
        pad_ref[pl.ds(0, steps), pl.ds(head * width, width)] = part
    return pad_ref[...]


def widen(shards, kv_local, steps):
    count, (per_worker, width) = len(shards), shards[0].shape
    row = lax.broadcasted_iota(jnp.int32, (count * per_worker, 1), 0)
    head = row % per_worker // (per_worker // kv_local)
    rows = jnp.concatenate([shard.astype(jnp.float32) for shard in shards], axis=0)
    wide = jnp.concatenate([jnp.where(head == k, rows, 0.0) for k in range(kv_local)], axis=1)
    return wide.astype(jnp.bfloat16), row % steps, head


def score(queries, keys, limit, begin):
    scores = jnp.dot(queries, keys, preferred_element_type=jnp.float32)
    column = lax.broadcasted_iota(jnp.int32, scores.shape, 1)
    return jnp.where(column < limit - begin, scores, masked_score)


def weigh(scores, scale):
    top = functools.reduce(jnp.maximum, [jnp.max(part, axis=1, keepdims=True) for part in scores])
    top = (top * scale).astype(jnp.bfloat16).astype(jnp.float32)
    weights = [jnp.exp2(part * scale - top) for part in scores]
    total = sum(jnp.sum(part, axis=1, keepdims=True) for part in weights)
    return [part.astype(jnp.bfloat16) for part in weights], top, total


def own_columns(both, head, kv_local):
    width = both.shape[1] // kv_local
    outputs = both[:, :width]
    for k in range(1, kv_local):
        outputs = jnp.where(head == k, both[:, k * width : (k + 1) * width], outputs)
    return outputs


def to_lanes(column):
    rows = column.shape[0]
    shape = (rows, lane_width)
    here = lax.broadcasted_iota(jnp.int32, shape, 0) == lax.broadcasted_iota(jnp.int32, shape, 1)
    return jnp.sum(jnp.where(here, column, 0.0), axis=0, keepdims=True)


def to_column(line, rows):
    shape = (rows, lane_width)
    here = lax.broadcasted_iota(jnp.int32, shape, 0) == lax.broadcasted_iota(jnp.int32, shape, 1)
    return jnp.sum(jnp.where(here, line, 0.0), axis=1, keepdims=True)


def pack(outputs, top, total):
    high = total.astype(jnp.bfloat16).astype(jnp.float32)
    top_line, high_line, low_line = to_lanes(top), to_lanes(high), to_lanes(total - high)
    line = lax.broadcasted_iota(jnp.int32, (stat_rows, lane_width), 0)
    stats = jnp.where(line == 0, top_line, jnp.where(line == 1, high_line, low_line))
    return jnp.concatenate([outputs, stats], axis=0).astype(jnp.bfloat16)


def first_kernel(
    kv_local, steps, chunks, lengths_hbm, query_hbm, cache_keys_hbm, cache_values_hbm, new_keys_hbm,
    new_values_hbm, keys_ref, values_ref, limits_ref, outputs_ref, stats_ref, lengths_ref, query_ref,
    raw_keys_ref, raw_values_ref, new_ref, wide_ref, small_ref, pad_ref, cache_sem, small_sem,
):
    size = raw_keys_ref.shape[0] // chunks
    span = size // kv_local
    width = query_ref.shape[1]
    slots = values_ref.shape[0] - lane_width
    scale = width ** (-0.5) * math.log2(math.e)
    fetch = [
        [
            pltpu.make_async_copy(
                source.at[pl.ds(i * size, size)], target.at[pl.ds(i * size, size)], cache_sem.at[side, i]
            )
            for i in range(chunks)
        ]
        for side, (source, target) in enumerate(
            ((cache_keys_hbm, raw_keys_ref), (cache_values_hbm, raw_values_ref))
        )
    ]
    small = [
        pltpu.make_async_copy(lengths_hbm, lengths_ref, small_sem.at[0]),
        pltpu.make_async_copy(query_hbm, query_ref, small_sem.at[1]),
        pltpu.make_async_copy(new_keys_hbm, new_ref.at[0], small_sem.at[2]),
        pltpu.make_async_copy(new_values_hbm, new_ref.at[1], small_sem.at[3]),
    ]
    for copy in small + fetch[0] + fetch[1]:
        copy.start()
    for copy in small:
        copy.wait()
    queries, step, head = widen([query_ref[...]], kv_local, steps)
    limit = jnp.zeros(step.shape, jnp.int32)
    for t in range(steps):
        limit = jnp.where(step == t, lengths_ref[0, t], limit)
    limits_ref[...] = jnp.broadcast_to(limit, limits_ref.shape)
    fresh_keys = pad_fresh(new_ref.at[0], small_ref.at[0], pad_ref.at[0], kv_local)
    fresh_values = pad_fresh(new_ref.at[1], small_ref.at[1], pad_ref.at[1], kv_local)
    keys_ref[:, pl.ds(slots, lane_width)] = fresh_keys.T.astype(jnp.bfloat16)
    values_ref[pl.ds(slots, lane_width), :] = fresh_values.astype(jnp.bfloat16)
    scores = [score(queries, keys_ref[:, pl.ds(slots, lane_width)], step + 1, 0)]
    for i in range(chunks):
        fetch[0][i].wait()
        part, columns = pl.ds(i * size, size), pl.ds(i * span, span)
        for k, picked in enumerate(pick_head(raw_keys_ref.at[part], wide_ref.at[0, part], kv_local)):
            keys_ref[pl.ds(k * width, width), columns] = picked.T.astype(jnp.bfloat16)
        scores.append(score(queries, keys_ref[:, columns], limit, i * span))
    weights, top, total = weigh(scores, scale)
    both = jnp.dot(
        weights[0], values_ref[pl.ds(slots, lane_width), :], preferred_element_type=jnp.float32
    )
    for i in range(chunks):
        fetch[1][i].wait()
        part, lines = pl.ds(i * size, size), pl.ds(i * span, span)
        for k, picked in enumerate(pick_head(raw_values_ref.at[part], wide_ref.at[1, part], kv_local)):
            values_ref[lines, pl.ds(k * width, width)] = picked.astype(jnp.bfloat16)
        both += jnp.dot(weights[i + 1], values_ref[lines, :], preferred_element_type=jnp.float32)
    outputs_ref[...] = own_columns(both, head, kv_local)
    lane = lax.broadcasted_iota(jnp.int32, stats_ref.shape, 1)
    stats_ref[...] = jnp.where(lane == 0, top, total)


def other_kernel(kv_local, steps, count, limits_ref, *refs):
    shards, (keys_ref, values_ref), packets = refs[:count], refs[count : count + 2], refs[count + 2 :]
    rows, width = shards[0].shape
    slots = values_ref.shape[0] - lane_width
    scale = width ** (-0.5) * math.log2(math.e)
    queries, step, head = widen([shard[...] for shard in shards], kv_local, steps)
    limit = jnp.concatenate([limits_ref[:, 0:1]] * count, axis=0)
    scores = [
        score(queries, keys_ref[:, pl.ds(0, slots)], limit, 0),
        score(queries, keys_ref[:, pl.ds(slots, lane_width)], step, 0),
    ]
    weights, top, total = weigh(scores, scale)
    both = jnp.dot(
        jnp.concatenate(weights, axis=1), values_ref[...], preferred_element_type=jnp.float32
    )
    results = (own_columns(both, head, kv_local), top, total)
    for place, packet_ref in enumerate(packets):
        packet_ref[...] = pack(*[part[place * rows : (place + 1) * rows] for part in results])


def merge_kernel(rows, outputs_ref, stats_ref, *refs):
    packets, merged_ref = refs[:-1], refs[-1]
    stats = stats_ref[...]
    parts = [(outputs_ref[...], stats[:, 0:1], stats[:, 1:2])]
    for packet_ref in packets:
        packet = packet_ref[...].astype(jnp.float32)
        lines = packet[rows : rows + stat_rows]
        parts.append(
            (
                packet[:rows],
                to_column(lines[0:1], rows),
                to_column(lines[1:2] + lines[2:3], rows),
            )
        )
    highest = functools.reduce(jnp.maximum, [top for _, top, _ in parts])
    factors = [jnp.exp2(top - highest) for _, top, _ in parts]
    total = sum(factor * part[2] for factor, part in zip(factors, parts))
    merged = sum(factor * part[0] for factor, part in zip(factors, parts))
    merged_ref[...] = (merged / total).astype(merged_ref.dtype)


vmem = pl.BlockSpec(memory_space=pltpu.VMEM)
hbm = pl.BlockSpec(memory_space=pltpu.HBM)
grant = 40 * 1024 * 1024


def shift(shard, offset, workers):
    return lax.ppermute(shard, "worker", [(i, (i + offset) % workers) for i in range(workers)])


def local(queries, cache_keys, cache_values, new_keys, new_values, lengths):
    _, steps, heads, width = queries.shape
    slots, kv_local = cache_keys.shape[1:3]
    rows = steps * heads
    workers = lax.axis_size("worker")
    chunks = max(1, slots // 512)
    flat = lambda cache: cache.reshape(-1, width)
    as_rows = lambda q: q[0].transpose(1, 0, 2).reshape(rows, width)
    packet = jax.ShapeDtypeStruct((rows + stat_rows, width), jnp.bfloat16)

    def first(query_rows):
        return pl.pallas_call(
            functools.partial(first_kernel, kv_local, steps, chunks),
            out_shape=(
                jax.ShapeDtypeStruct((kv_local * width, slots + lane_width), jnp.bfloat16),
                jax.ShapeDtypeStruct((slots + lane_width, kv_local * width), jnp.bfloat16),
                jax.ShapeDtypeStruct((rows, lane_width), jnp.int32),
                jax.ShapeDtypeStruct((rows, width), jnp.float32),
                jax.ShapeDtypeStruct((rows, lane_width), jnp.float32),
            ),
            in_specs=[hbm] * 6,
            out_specs=(vmem,) * 5,
            scratch_shapes=[
                pltpu.SMEM((1, steps), jnp.int32),
                pltpu.VMEM((rows, width), jnp.bfloat16),
                pltpu.VMEM((slots * kv_local, width), jnp.bfloat16),
                pltpu.VMEM((slots * kv_local, width), jnp.bfloat16),
                pltpu.VMEM((2, steps * kv_local, width), jnp.bfloat16),
                pltpu.VMEM((2, slots * kv_local, width), jnp.float32),
                pltpu.VMEM((2, steps * kv_local, width), jnp.float32),
                pltpu.VMEM((2, lane_width, kv_local * width), jnp.float32),
                pltpu.SemaphoreType.DMA((2, chunks)),
                pltpu.SemaphoreType.DMA((4,)),
            ],
            compiler_params=pltpu.CompilerParams(vmem_limit_bytes=grant),
            name="own_rows",
        )(
            *[
                pltpu.with_memory_space_constraint(x, pltpu.HBM)
                for x in (lengths, query_rows, flat(cache_keys), flat(cache_values), flat(new_keys), flat(new_values))
            ],
        )

    def others(query_list, keys, values, limits):
        count = len(query_list)
        return pl.pallas_call(
            functools.partial(other_kernel, kv_local, steps, count),
            out_shape=(packet,) * count,
            in_specs=[vmem] * (count + 3),
            out_specs=(vmem,) * count,
            compiler_params=pltpu.CompilerParams(vmem_limit_bytes=grant),
            name="partner_rows",
        )(limits, *query_list, keys, values)

    def merge(outputs, stats, packets):
        return pl.pallas_call(
            functools.partial(merge_kernel, rows),
            out_shape=jax.ShapeDtypeStruct((rows, width), jnp.bfloat16),
            in_specs=[vmem] * (2 + len(packets)),
            out_specs=vmem,
            compiler_params=pltpu.CompilerParams(vmem_limit_bytes=grant // 10),
            name="merge",
        )(outputs, stats, *packets)

    arrived = [as_rows(shift(queries, offset, workers)) for offset in range(1, workers)]
    keys, values, limits, outputs, stats = first(as_rows(queries))
    sent = others(arrived, keys, values, limits) if arrived else ()
    packets = [shift(sent[workers - 1 - offset], offset, workers) for offset in range(1, workers)]
    merged = merge(outputs, stats, packets)
    return merged.reshape(heads, steps, width).transpose(1, 0, 2)[None]


def solution(mesh):
    split = P(("problem", "worker"), None, "head", None)
    return jax.shard_map(
        local,
        mesh=mesh,
        in_specs=(split,) * 5 + (P(("problem", "worker"), None),),
        out_specs=split,
        check_vma=False,
    )
```

```python
import functools
import math

import jax
import jax.numpy as jnp
from jax import lax
from jax.experimental import pallas as pl
from jax.experimental.pallas import tpu as pltpu
from jax.sharding import PartitionSpec as P

masked_score = -1e30
lane_width = 128
stat_rows = 8


def pick_head(source_ref, wide_ref, kv_local):
    slots = source_ref.shape[0] // kv_local
    wide_ref[...] = source_ref[...].astype(jnp.float32)
    return [wide_ref[pl.ds(head, slots, stride=kv_local), :] for head in range(kv_local)]


def pad_fresh(source_ref, wide_ref, pad_ref, kv_local):
    parts = pick_head(source_ref, wide_ref, kv_local)
    steps, width = parts[0].shape
    pad_ref[...] = jnp.zeros_like(pad_ref)
    for head, part in enumerate(parts):
        pad_ref[pl.ds(0, steps), pl.ds(head * width, width)] = part
    return pad_ref[...]


def widen(shards, kv_local, steps):
    count, (per_worker, width) = len(shards), shards[0].shape
    row = lax.broadcasted_iota(jnp.int32, (count * per_worker, 1), 0)
    head = row % per_worker // (per_worker // kv_local)
    rows = jnp.concatenate([shard.astype(jnp.float32) for shard in shards], axis=0)
    wide = jnp.concatenate([jnp.where(head == k, rows, 0.0) for k in range(kv_local)], axis=1)
    return wide.astype(jnp.bfloat16), row % steps, head


def score(queries, keys, limit):
    scores = jnp.dot(queries, keys, preferred_element_type=jnp.float32)
    column = lax.broadcasted_iota(jnp.int32, scores.shape, 1)
    return jnp.where(column < limit, scores, masked_score)


def weigh(scores, scale):
    top = functools.reduce(jnp.maximum, [jnp.max(part, axis=1, keepdims=True) for part in scores])
    top = (top * scale).astype(jnp.bfloat16).astype(jnp.float32)
    weights = [jnp.exp2(part * scale - top) for part in scores]
    total = sum(jnp.sum(part, axis=1, keepdims=True) for part in weights)
    return [part.astype(jnp.bfloat16) for part in weights], top, total


def own_columns(both, head, kv_local):
    width = both.shape[1] // kv_local
    outputs = both[:, :width]
    for k in range(1, kv_local):
        outputs = jnp.where(head == k, both[:, k * width : (k + 1) * width], outputs)
    return outputs


def to_lanes(column):
    rows = column.shape[0]
    shape = (rows, lane_width)
    here = lax.broadcasted_iota(jnp.int32, shape, 0) == lax.broadcasted_iota(jnp.int32, shape, 1)
    return jnp.sum(jnp.where(here, column, 0.0), axis=0, keepdims=True)


def to_column(line, rows):
    shape = (rows, lane_width)
    here = lax.broadcasted_iota(jnp.int32, shape, 0) == lax.broadcasted_iota(jnp.int32, shape, 1)
    return jnp.sum(jnp.where(here, line, 0.0), axis=1, keepdims=True)


def pack(outputs, top, total):
    high = total.astype(jnp.bfloat16).astype(jnp.float32)
    top_line, high_line, low_line = to_lanes(top), to_lanes(high), to_lanes(total - high)
    line = lax.broadcasted_iota(jnp.int32, (stat_rows, lane_width), 0)
    stats = jnp.where(line == 0, top_line, jnp.where(line == 1, high_line, low_line))
    return jnp.concatenate([outputs, stats], axis=0).astype(jnp.bfloat16)


def prepare_kernel(
    kv_local, steps, chunks, lengths_hbm, cache_keys_hbm, cache_values_hbm, new_keys_hbm, new_values_hbm,
    keys_ref, values_ref, limits_ref, lengths_ref, raw_keys_ref, raw_values_ref, new_ref, wide_ref,
    small_ref, pad_ref, cache_sem, small_sem,
):
    size = raw_keys_ref.shape[0] // chunks
    span = size // kv_local
    width = raw_keys_ref.shape[1]
    slots = values_ref.shape[0] - lane_width
    fetch = [
        [
            pltpu.make_async_copy(
                source.at[pl.ds(i * size, size)], target.at[pl.ds(i * size, size)], cache_sem.at[side, i]
            )
            for i in range(chunks)
        ]
        for side, (source, target) in enumerate(
            ((cache_keys_hbm, raw_keys_ref), (cache_values_hbm, raw_values_ref))
        )
    ]
    small = [
        pltpu.make_async_copy(lengths_hbm, lengths_ref, small_sem.at[0]),
        pltpu.make_async_copy(new_keys_hbm, new_ref.at[0], small_sem.at[1]),
        pltpu.make_async_copy(new_values_hbm, new_ref.at[1], small_sem.at[2]),
    ]
    for copy in small + fetch[0] + fetch[1]:
        copy.start()
    for copy in small:
        copy.wait()
    step = lax.broadcasted_iota(jnp.int32, limits_ref.shape, 0) % steps
    limit = jnp.zeros(step.shape, jnp.int32)
    for t in range(steps):
        limit = jnp.where(step == t, lengths_ref[0, t], limit)
    limits_ref[...] = limit
    fresh_keys = pad_fresh(new_ref.at[0], small_ref.at[0], pad_ref.at[0], kv_local)
    fresh_values = pad_fresh(new_ref.at[1], small_ref.at[1], pad_ref.at[1], kv_local)
    keys_ref[:, pl.ds(slots, lane_width)] = fresh_keys.astype(jnp.bfloat16).T
    values_ref[pl.ds(slots, lane_width), :] = fresh_values.astype(jnp.bfloat16)
    for i in range(chunks):
        fetch[0][i].wait()
        part, columns = pl.ds(i * size, size), pl.ds(i * span, span)
        for k, picked in enumerate(pick_head(raw_keys_ref.at[part], wide_ref.at[0, part], kv_local)):
            keys_ref[pl.ds(k * width, width), columns] = picked.astype(jnp.bfloat16).T
    for i in range(chunks):
        fetch[1][i].wait()
        part, lines = pl.ds(i * size, size), pl.ds(i * span, span)
        for k, picked in enumerate(pick_head(raw_values_ref.at[part], wide_ref.at[1, part], kv_local)):
            values_ref[lines, pl.ds(k * width, width)] = picked.astype(jnp.bfloat16)


def attend(shards, keys_ref, values_ref, limits_ref, kv_local, steps, own):
    count, width = len(shards), shards[0].shape[1]
    slots = values_ref.shape[0] - lane_width
    scale = width ** (-0.5) * math.log2(math.e)
    queries, step, head = widen(shards, kv_local, steps)
    limit = jnp.concatenate([limits_ref[:, 0:1]] * count, axis=0)
    scores = [
        score(queries, keys_ref[:, pl.ds(0, slots)], limit),
        score(queries, keys_ref[:, pl.ds(slots, lane_width)], step + 1 if own else step),
    ]
    weights, top, total = weigh(scores, scale)
    begins = (0, slots)
    outputs = None
    for k in range(kv_local):
        columns = pl.ds(k * width, width)
        part = sum(
            jnp.dot(part, values_ref[pl.ds(begin, part.shape[1]), columns], preferred_element_type=jnp.float32)
            for part, begin in zip(weights, begins)
        )
        outputs = part if outputs is None else jnp.where(head == k, part, outputs)
    return outputs, top, total


def own_kernel(kv_local, steps, keys_ref, values_ref, limits_ref, query_ref, outputs_ref, stats_ref):
    outputs, top, total = attend(
        [query_ref[...]], keys_ref, values_ref, limits_ref, kv_local, steps, True
    )
    outputs_ref[...] = outputs
    lane = lax.broadcasted_iota(jnp.int32, stats_ref.shape, 1)
    stats_ref[...] = jnp.where(lane == 0, top, total)


def partner_kernel(kv_local, steps, count, keys_ref, values_ref, limits_ref, *refs):
    shards, packets = refs[:count], refs[count:]
    rows = shards[0].shape[0]
    results = attend(
        [shard[...] for shard in shards], keys_ref, values_ref, limits_ref, kv_local, steps, False
    )
    for place, packet_ref in enumerate(packets):
        packet_ref[...] = pack(*[part[place * rows : (place + 1) * rows] for part in results])


def merge_kernel(rows, outputs_ref, stats_ref, *refs):
    packets, merged_ref = refs[:-1], refs[-1]
    stats = stats_ref[...]
    parts = [(outputs_ref[...], stats[:, 0:1], stats[:, 1:2])]
    for packet_ref in packets:
        packet = packet_ref[...].astype(jnp.float32)
        lines = packet[rows : rows + stat_rows]
        parts.append(
            (
                packet[:rows],
                to_column(lines[0:1], rows),
                to_column(lines[1:2] + lines[2:3], rows),
            )
        )
    highest = functools.reduce(jnp.maximum, [top for _, top, _ in parts])
    factors = [jnp.exp2(top - highest) for _, top, _ in parts]
    total = sum(factor * part[2] for factor, part in zip(factors, parts))
    merged = sum(factor * part[0] for factor, part in zip(factors, parts))
    merged_ref[...] = (merged / total).astype(merged_ref.dtype)


vmem = pl.BlockSpec(memory_space=pltpu.VMEM)
hbm = pl.BlockSpec(memory_space=pltpu.HBM)
grant = 40 * 1024 * 1024


def shift(shard, offset, workers):
    return lax.ppermute(shard, "worker", [(i, (i + offset) % workers) for i in range(workers)])


def local(queries, cache_keys, cache_values, new_keys, new_values, lengths):
    _, steps, heads, width = queries.shape
    slots, kv_local = cache_keys.shape[1:3]
    rows = steps * heads
    workers = lax.axis_size("worker")
    chunks = max(1, slots // 1024)
    flat = lambda cache: cache.reshape(-1, width)
    as_rows = lambda q: q[0].transpose(1, 0, 2).reshape(rows, width)
    packet = jax.ShapeDtypeStruct((rows + stat_rows, width), jnp.bfloat16)

    def prepare():
        return pl.pallas_call(
            functools.partial(prepare_kernel, kv_local, steps, chunks),
            out_shape=(
                jax.ShapeDtypeStruct((kv_local * width, slots + lane_width), jnp.bfloat16),
                jax.ShapeDtypeStruct((slots + lane_width, kv_local * width), jnp.bfloat16),
                jax.ShapeDtypeStruct((rows, lane_width), jnp.int32),
            ),
            in_specs=[hbm] * 5,
            out_specs=(vmem,) * 3,
            scratch_shapes=[
                pltpu.SMEM((1, steps), jnp.int32),
                pltpu.VMEM((slots * kv_local, width), jnp.bfloat16),
                pltpu.VMEM((slots * kv_local, width), jnp.bfloat16),
                pltpu.VMEM((2, steps * kv_local, width), jnp.bfloat16),
                pltpu.VMEM((2, slots * kv_local, width), jnp.float32),
                pltpu.VMEM((2, steps * kv_local, width), jnp.float32),
                pltpu.VMEM((2, lane_width, kv_local * width), jnp.float32),
                pltpu.SemaphoreType.DMA((2, chunks)),
                pltpu.SemaphoreType.DMA((3,)),
            ],
            compiler_params=pltpu.CompilerParams(vmem_limit_bytes=grant),
            name="prepare",
        )(
            *[
                pltpu.with_memory_space_constraint(x, pltpu.HBM)
                for x in (lengths, flat(cache_keys), flat(cache_values), flat(new_keys), flat(new_values))
            ]
        )

    def own(prepared, query_rows):
        return pl.pallas_call(
            functools.partial(own_kernel, kv_local, steps),
            out_shape=(
                jax.ShapeDtypeStruct((rows, width), jnp.float32),
                jax.ShapeDtypeStruct((rows, lane_width), jnp.float32),
            ),
            in_specs=[vmem] * 4,
            out_specs=(vmem,) * 2,
            compiler_params=pltpu.CompilerParams(vmem_limit_bytes=grant),
            name="own_rows",
        )(*prepared, query_rows)

    def partners(prepared, query_list):
        count = len(query_list)
        return pl.pallas_call(
            functools.partial(partner_kernel, kv_local, steps, count),
            out_shape=(packet,) * count,
            in_specs=[vmem] * (count + 3),
            out_specs=(vmem,) * count,
            compiler_params=pltpu.CompilerParams(vmem_limit_bytes=grant),
            name="partner_rows",
        )(*prepared, *query_list)

    def merge(outputs, stats, packets):
        return pl.pallas_call(
            functools.partial(merge_kernel, rows),
            out_shape=jax.ShapeDtypeStruct((rows, width), jnp.bfloat16),
            in_specs=[vmem] * (2 + len(packets)),
            out_specs=vmem,
            compiler_params=pltpu.CompilerParams(vmem_limit_bytes=grant // 10),
            name="merge",
        )(outputs, stats, *packets)

    middle = workers // 2
    offsets = [middle] + [offset for offset in range(1, workers) if offset != middle]
    arrived = [as_rows(shift(queries, offset, workers)) for offset in offsets]
    prepared = prepare()
    sent = partners(prepared, arrived) if arrived else ()
    packets = [shift(sent[offsets.index(workers - offset)], offset, workers) for offset in range(1, workers)]
    outputs, stats = own(prepared, as_rows(queries))
    merged = merge(outputs, stats, packets)
    return merged.reshape(heads, steps, width).transpose(1, 0, 2)[None]


def solution(mesh):
    split = P(("problem", "worker"), None, "head", None)
    return jax.shard_map(
        local,
        mesh=mesh,
        in_specs=(split,) * 5 + (P(("problem", "worker"), None),),
        out_specs=split,
        check_vma=False,
    )
```

```python
import functools
import math

import jax
import jax.numpy as jnp
from jax import lax
from jax.experimental import pallas as pl
from jax.experimental.pallas import tpu as pltpu
from jax.sharding import PartitionSpec as P

masked_score = -1e30
lane_width = 128
stat_rows = 8


def pick_head(source_ref, wide_ref, kv_local):
    slots = source_ref.shape[0] // kv_local
    wide_ref[...] = source_ref[...].astype(jnp.float32)
    return [wide_ref[pl.ds(head, slots, stride=kv_local), :] for head in range(kv_local)]


def pad_fresh(source_ref, wide_ref, pad_ref, kv_local):
    parts = pick_head(source_ref, wide_ref, kv_local)
    steps, width = parts[0].shape
    pad_ref[...] = jnp.zeros_like(pad_ref)
    for head, part in enumerate(parts):
        pad_ref[pl.ds(0, steps), pl.ds(head * width, width)] = part
    return pad_ref[...]


def widen(shards, kv_local, steps):
    count, (per_worker, width) = len(shards), shards[0].shape
    row = lax.broadcasted_iota(jnp.int32, (count * per_worker, 1), 0)
    head = row % per_worker // (per_worker // kv_local)
    rows = jnp.concatenate([shard.astype(jnp.float32) for shard in shards], axis=0)
    wide = jnp.concatenate([jnp.where(head == k, rows, 0.0) for k in range(kv_local)], axis=1)
    return wide.astype(jnp.bfloat16), row % steps, head


def score(queries, keys, limit):
    scores = jnp.dot(queries, keys, preferred_element_type=jnp.float32)
    column = lax.broadcasted_iota(jnp.int32, scores.shape, 1)
    return jnp.where(column < limit, scores, masked_score)


def weigh(scores, scale):
    top = functools.reduce(jnp.maximum, [jnp.max(part, axis=1, keepdims=True) for part in scores])
    top = (top * scale).astype(jnp.bfloat16).astype(jnp.float32)
    weights = [jnp.exp2(part * scale - top) for part in scores]
    total = sum(jnp.sum(part, axis=1, keepdims=True) for part in weights)
    return [part.astype(jnp.bfloat16) for part in weights], top, total


def own_columns(both, head, kv_local):
    width = both.shape[1] // kv_local
    outputs = both[:, :width]
    for k in range(1, kv_local):
        outputs = jnp.where(head == k, both[:, k * width : (k + 1) * width], outputs)
    return outputs


def to_lanes(column):
    rows = column.shape[0]
    shape = (rows, lane_width)
    here = lax.broadcasted_iota(jnp.int32, shape, 0) == lax.broadcasted_iota(jnp.int32, shape, 1)
    return jnp.sum(jnp.where(here, column, 0.0), axis=0, keepdims=True)


def to_column(line, rows):
    shape = (rows, lane_width)
    here = lax.broadcasted_iota(jnp.int32, shape, 0) == lax.broadcasted_iota(jnp.int32, shape, 1)
    return jnp.sum(jnp.where(here, line, 0.0), axis=1, keepdims=True)


def pack(outputs, top, total):
    high = total.astype(jnp.bfloat16).astype(jnp.float32)
    top_line, high_line, low_line = to_lanes(top), to_lanes(high), to_lanes(total - high)
    line = lax.broadcasted_iota(jnp.int32, (stat_rows, lane_width), 0)
    stats = jnp.where(line == 0, top_line, jnp.where(line == 1, high_line, low_line))
    return jnp.concatenate([outputs, stats], axis=0).astype(jnp.bfloat16)


def prepare_kernel(
    kv_local, steps, chunks, lengths_hbm, cache_keys_hbm, cache_values_hbm, new_keys_hbm, new_values_hbm,
    keys_ref, values_ref, limits_ref, lengths_ref, raw_keys_ref, raw_values_ref, new_ref, wide_ref,
    small_ref, pad_ref, cache_sem, small_sem,
):
    size = raw_keys_ref.shape[0] // chunks
    span = size // kv_local
    width = raw_keys_ref.shape[1]
    slots = values_ref.shape[0] - lane_width
    fetch = [
        [
            pltpu.make_async_copy(
                source.at[pl.ds(i * size, size)], target.at[pl.ds(i * size, size)], cache_sem.at[side, i]
            )
            for i in range(chunks)
        ]
        for side, (source, target) in enumerate(
            ((cache_keys_hbm, raw_keys_ref), (cache_values_hbm, raw_values_ref))
        )
    ]
    small = [
        pltpu.make_async_copy(lengths_hbm, lengths_ref, small_sem.at[0]),
        pltpu.make_async_copy(new_keys_hbm, new_ref.at[0], small_sem.at[1]),
        pltpu.make_async_copy(new_values_hbm, new_ref.at[1], small_sem.at[2]),
    ]
    for copy in small + fetch[0] + fetch[1]:
        copy.start()
    for copy in small:
        copy.wait()
    step = lax.broadcasted_iota(jnp.int32, limits_ref.shape, 0) % steps
    limit = jnp.zeros(step.shape, jnp.int32)
    for t in range(steps):
        limit = jnp.where(step == t, lengths_ref[0, t], limit)
    limits_ref[...] = limit
    fresh_keys = pad_fresh(new_ref.at[0], small_ref.at[0], pad_ref.at[0], kv_local)
    fresh_values = pad_fresh(new_ref.at[1], small_ref.at[1], pad_ref.at[1], kv_local)
    keys_ref[:, pl.ds(slots, lane_width)] = fresh_keys.astype(jnp.bfloat16).T
    values_ref[pl.ds(slots, lane_width), :] = fresh_values.astype(jnp.bfloat16)
    for i in range(chunks):
        fetch[0][i].wait()
        part, columns = pl.ds(i * size, size), pl.ds(i * span, span)
        for k, picked in enumerate(pick_head(raw_keys_ref.at[part], wide_ref.at[0, part], kv_local)):
            keys_ref[pl.ds(k * width, width), columns] = picked.astype(jnp.bfloat16).T
    for i in range(chunks):
        fetch[1][i].wait()
        part, lines = pl.ds(i * size, size), pl.ds(i * span, span)
        for k, picked in enumerate(pick_head(raw_values_ref.at[part], wide_ref.at[1, part], kv_local)):
            values_ref[lines, pl.ds(k * width, width)] = picked.astype(jnp.bfloat16)


def attend(shards, keys_ref, values_ref, limits_ref, kv_local, steps, own):
    count, width = len(shards), shards[0].shape[1]
    slots = values_ref.shape[0] - lane_width
    scale = width ** (-0.5) * math.log2(math.e)
    queries, step, head = widen(shards, kv_local, steps)
    limit = jnp.concatenate([limits_ref[:, 0:1]] * count, axis=0)
    scores = [
        score(queries, keys_ref[:, pl.ds(0, slots)], limit),
        score(queries, keys_ref[:, pl.ds(slots, lane_width)], step + 1 if own else step),
    ]
    weights, top, total = weigh(scores, scale)
    begins = (0, slots)
    outputs = None
    for k in range(kv_local):
        columns = pl.ds(k * width, width)
        part = sum(
            jnp.dot(part, values_ref[pl.ds(begin, part.shape[1]), columns], preferred_element_type=jnp.float32)
            for part, begin in zip(weights, begins)
        )
        outputs = part if outputs is None else jnp.where(head == k, part, outputs)
    return outputs, top, total


def own_kernel(kv_local, steps, keys_ref, values_ref, limits_ref, query_ref, outputs_ref, stats_ref):
    outputs, top, total = attend(
        [query_ref[...]], keys_ref, values_ref, limits_ref, kv_local, steps, True
    )
    outputs_ref[...] = outputs
    lane = lax.broadcasted_iota(jnp.int32, stats_ref.shape, 1)
    stats_ref[...] = jnp.where(lane == 0, top, total)


def partner_kernel(kv_local, steps, count, keys_ref, values_ref, limits_ref, *refs):
    shards, packets = refs[:count], refs[count:]
    rows = shards[0].shape[0]
    results = attend(
        [shard[...] for shard in shards], keys_ref, values_ref, limits_ref, kv_local, steps, False
    )
    for place, packet_ref in enumerate(packets):
        packet_ref[...] = pack(*[part[place * rows : (place + 1) * rows] for part in results])


def merge_parts(rows, outputs_ref, stats_ref, packets):
    stats = stats_ref[...]
    parts = [(outputs_ref[...], stats[:, 0:1], stats[:, 1:2])]
    for packet_ref in packets:
        packet = packet_ref[...].astype(jnp.float32)
        lines = packet[rows : rows + stat_rows]
        parts.append(
            (
                packet[:rows],
                to_column(lines[0:1], rows),
                to_column(lines[1:2] + lines[2:3], rows),
            )
        )
    highest = functools.reduce(jnp.maximum, [top for _, top, _ in parts])
    factors = [jnp.exp2(top - highest) for _, top, _ in parts]
    total = sum(factor * part[2] for factor, part in zip(factors, parts))
    merged = sum(factor * part[0] for factor, part in zip(factors, parts))
    return merged, highest, total


def fold_kernel(rows, outputs_ref, stats_ref, *refs):
    packets, (folded_ref, folded_stats_ref) = refs[:-2], refs[-2:]
    merged, highest, total = merge_parts(rows, outputs_ref, stats_ref, packets)
    folded_ref[...] = merged
    lane = lax.broadcasted_iota(jnp.int32, folded_stats_ref.shape, 1)
    folded_stats_ref[...] = jnp.where(lane == 0, highest, total)


def merge_kernel(rows, outputs_ref, stats_ref, *refs):
    packets, merged_ref = refs[:-1], refs[-1]
    merged, _, total = merge_parts(rows, outputs_ref, stats_ref, packets)
    merged_ref[...] = (merged / total).astype(merged_ref.dtype)


vmem = pl.BlockSpec(memory_space=pltpu.VMEM)
hbm = pl.BlockSpec(memory_space=pltpu.HBM)
grant = 40 * 1024 * 1024


def shift(shard, offset, workers):
    return lax.ppermute(shard, "worker", [(i, (i + offset) % workers) for i in range(workers)])


def local(queries, cache_keys, cache_values, new_keys, new_values, lengths):
    _, steps, heads, width = queries.shape
    slots, kv_local = cache_keys.shape[1:3]
    rows = steps * heads
    workers = lax.axis_size("worker")
    chunks = max(1, slots // 1024)
    flat = lambda cache: cache.reshape(-1, width)
    as_rows = lambda q: q[0].transpose(1, 0, 2).reshape(rows, width)
    packet = jax.ShapeDtypeStruct((rows + stat_rows, width), jnp.bfloat16)

    def prepare():
        return pl.pallas_call(
            functools.partial(prepare_kernel, kv_local, steps, chunks),
            out_shape=(
                jax.ShapeDtypeStruct((kv_local * width, slots + lane_width), jnp.bfloat16),
                jax.ShapeDtypeStruct((slots + lane_width, kv_local * width), jnp.bfloat16),
                jax.ShapeDtypeStruct((rows, lane_width), jnp.int32),
            ),
            in_specs=[hbm] * 5,
            out_specs=(vmem,) * 3,
            scratch_shapes=[
                pltpu.SMEM((1, steps), jnp.int32),
                pltpu.VMEM((slots * kv_local, width), jnp.bfloat16),
                pltpu.VMEM((slots * kv_local, width), jnp.bfloat16),
                pltpu.VMEM((2, steps * kv_local, width), jnp.bfloat16),
                pltpu.VMEM((2, slots * kv_local, width), jnp.float32),
                pltpu.VMEM((2, steps * kv_local, width), jnp.float32),
                pltpu.VMEM((2, lane_width, kv_local * width), jnp.float32),
                pltpu.SemaphoreType.DMA((2, chunks)),
                pltpu.SemaphoreType.DMA((3,)),
            ],
            compiler_params=pltpu.CompilerParams(vmem_limit_bytes=grant),
            name="prepare",
        )(
            *[
                pltpu.with_memory_space_constraint(x, pltpu.HBM)
                for x in (lengths, flat(cache_keys), flat(cache_values), flat(new_keys), flat(new_values))
            ]
        )

    def own(prepared, query_rows):
        return pl.pallas_call(
            functools.partial(own_kernel, kv_local, steps),
            out_shape=(
                jax.ShapeDtypeStruct((rows, width), jnp.float32),
                jax.ShapeDtypeStruct((rows, lane_width), jnp.float32),
            ),
            in_specs=[vmem] * 4,
            out_specs=(vmem,) * 2,
            compiler_params=pltpu.CompilerParams(vmem_limit_bytes=grant),
            name="own_rows",
        )(*prepared, query_rows)

    def partners(prepared, query_list):
        count = len(query_list)
        return pl.pallas_call(
            functools.partial(partner_kernel, kv_local, steps, count),
            out_shape=(packet,) * count,
            in_specs=[vmem] * (count + 3),
            out_specs=(vmem,) * count,
            compiler_params=pltpu.CompilerParams(vmem_limit_bytes=grant),
            name="partner_rows",
        )(*prepared, *query_list)

    def fold(outputs, stats, packets):
        return pl.pallas_call(
            functools.partial(fold_kernel, rows),
            out_shape=(
                jax.ShapeDtypeStruct((rows, width), jnp.float32),
                jax.ShapeDtypeStruct((rows, lane_width), jnp.float32),
            ),
            in_specs=[vmem] * (2 + len(packets)),
            out_specs=(vmem,) * 2,
            compiler_params=pltpu.CompilerParams(vmem_limit_bytes=grant // 10),
            name="fold",
        )(outputs, stats, *packets)

    def merge(outputs, stats, packets):
        return pl.pallas_call(
            functools.partial(merge_kernel, rows),
            out_shape=jax.ShapeDtypeStruct((rows, width), jnp.bfloat16),
            in_specs=[vmem] * (2 + len(packets)),
            out_specs=vmem,
            compiler_params=pltpu.CompilerParams(vmem_limit_bytes=grant // 10),
            name="merge",
        )(outputs, stats, *packets)

    offsets = list(range(1, workers))
    middle = workers // 2
    arrived = {offset: as_rows(shift(queries, offset, workers)) for offset in offsets}
    prepared = prepare()
    sent = {}
    for group in ([offset for offset in offsets if offset != middle], offsets[middle - 1 : middle]):
        if group:
            sent |= dict(zip(group, partners(prepared, [arrived[offset] for offset in group])))
    packets = [shift(sent[workers - offset], offset, workers) for offset in offsets]
    outputs, stats = own(prepared, as_rows(queries))
    stages = [stage for stage in (packets[:1], packets[1:-1], packets[1:][-1:]) if stage]
    for stage in stages[:-1]:
        outputs, stats = fold(outputs, stats, stage)
    merged = merge(outputs, stats, stages[-1] if stages else [])
    return merged.reshape(heads, steps, width).transpose(1, 0, 2)[None]


def solution(mesh):
    split = P(("problem", "worker"), None, "head", None)
    return jax.shard_map(
        local,
        mesh=mesh,
        in_specs=(split,) * 5 + (P(("problem", "worker"), None),),
        out_specs=split,
        check_vma=False,
    )
```

```python
import functools
import math

import jax
import jax.numpy as jnp
from jax import lax
from jax.experimental import pallas as pl
from jax.experimental.pallas import tpu as pltpu
from jax.sharding import PartitionSpec as P

masked_score = -1e30
lane_width = 128
stat_rows = 8


def pick_head(source_ref, wide_ref, kv_local):
    slots = source_ref.shape[0] // kv_local
    wide_ref[...] = source_ref[...].astype(jnp.float32)
    return [wide_ref[pl.ds(head, slots, stride=kv_local), :] for head in range(kv_local)]


def pad_fresh(source_ref, wide_ref, pad_ref, kv_local):
    parts = pick_head(source_ref, wide_ref, kv_local)
    steps, width = parts[0].shape
    pad_ref[...] = jnp.zeros_like(pad_ref)
    for head, part in enumerate(parts):
        pad_ref[pl.ds(0, steps), pl.ds(head * width, width)] = part
    return pad_ref[...]


def stack(shards, kv_local, steps):
    count, per_worker = len(shards), shards[0].shape[0]
    row = lax.broadcasted_iota(jnp.int32, (count * per_worker, 1), 0)
    head = row % per_worker // (per_worker // kv_local)
    rows = jnp.concatenate([shard.astype(jnp.float32) for shard in shards], axis=0)
    return rows.astype(jnp.bfloat16), row % steps, head


def score(queries, head, keys, limit):
    width = queries.shape[1]
    scores = None
    for k in range(keys.shape[0] // width):
        part = jnp.dot(queries, keys[k * width : (k + 1) * width], preferred_element_type=jnp.float32)
        scores = part if scores is None else jnp.where(head == k, part, scores)
    column = lax.broadcasted_iota(jnp.int32, scores.shape, 1)
    return jnp.where(column < limit, scores, masked_score)


def weigh(scores, scale):
    top = functools.reduce(jnp.maximum, [jnp.max(part, axis=1, keepdims=True) for part in scores])
    top = (top * scale).astype(jnp.bfloat16).astype(jnp.float32)
    weights = [jnp.exp2(part * scale - top) for part in scores]
    total = sum(jnp.sum(part, axis=1, keepdims=True) for part in weights)
    return [part.astype(jnp.bfloat16) for part in weights], top, total


def to_lanes(column):
    rows = column.shape[0]
    shape = (rows, lane_width)
    here = lax.broadcasted_iota(jnp.int32, shape, 0) == lax.broadcasted_iota(jnp.int32, shape, 1)
    return jnp.sum(jnp.where(here, column, 0.0), axis=0, keepdims=True)


def to_column(line, rows):
    shape = (rows, lane_width)
    here = lax.broadcasted_iota(jnp.int32, shape, 0) == lax.broadcasted_iota(jnp.int32, shape, 1)
    return jnp.sum(jnp.where(here, line, 0.0), axis=1, keepdims=True)


def pack(outputs, top, total):
    high = total.astype(jnp.bfloat16).astype(jnp.float32)
    top_line, high_line, low_line = to_lanes(top), to_lanes(high), to_lanes(total - high)
    line = lax.broadcasted_iota(jnp.int32, (stat_rows, lane_width), 0)
    stats = jnp.where(line == 0, top_line, jnp.where(line == 1, high_line, low_line))
    return jnp.concatenate([outputs, stats], axis=0).astype(jnp.bfloat16)


def prepare_kernel(
    kv_local, steps, chunks, lengths_hbm, cache_keys_hbm, cache_values_hbm, new_keys_hbm, new_values_hbm,
    keys_ref, values_ref, limits_ref, lengths_ref, raw_keys_ref, raw_values_ref, new_ref, wide_ref,
    small_ref, pad_ref, cache_sem, small_sem,
):
    size = raw_keys_ref.shape[0] // chunks
    span = size // kv_local
    width = raw_keys_ref.shape[1]
    slots = values_ref.shape[0] - lane_width
    fetch = [
        [
            pltpu.make_async_copy(
                source.at[pl.ds(i * size, size)], target.at[pl.ds(i * size, size)], cache_sem.at[side, i]
            )
            for i in range(chunks)
        ]
        for side, (source, target) in enumerate(
            ((cache_keys_hbm, raw_keys_ref), (cache_values_hbm, raw_values_ref))
        )
    ]
    small = [
        pltpu.make_async_copy(lengths_hbm, lengths_ref, small_sem.at[0]),
        pltpu.make_async_copy(new_keys_hbm, new_ref.at[0], small_sem.at[1]),
        pltpu.make_async_copy(new_values_hbm, new_ref.at[1], small_sem.at[2]),
    ]
    for copy in small + fetch[0] + fetch[1]:
        copy.start()
    for i in range(chunks):
        fetch[0][i].wait()
        part, columns = pl.ds(i * size, size), pl.ds(i * span, span)
        for k, picked in enumerate(pick_head(raw_keys_ref.at[part], wide_ref.at[0, part], kv_local)):
            keys_ref[pl.ds(k * width, width), columns] = picked.astype(jnp.bfloat16).T
    for copy in small:
        copy.wait()
    step = lax.broadcasted_iota(jnp.int32, limits_ref.shape, 0) % steps
    limit = jnp.zeros(step.shape, jnp.int32)
    for t in range(steps):
        limit = jnp.where(step == t, lengths_ref[0, t], limit)
    limits_ref[...] = limit
    fresh_keys = pad_fresh(new_ref.at[0], small_ref.at[0], pad_ref.at[0], kv_local)
    fresh_values = pad_fresh(new_ref.at[1], small_ref.at[1], pad_ref.at[1], kv_local)
    keys_ref[:, pl.ds(slots, lane_width)] = fresh_keys.astype(jnp.bfloat16).T
    values_ref[pl.ds(slots, lane_width), :] = fresh_values.astype(jnp.bfloat16)
    for i in range(chunks):
        fetch[1][i].wait()
        part, lines = pl.ds(i * size, size), pl.ds(i * span, span)
        for k, picked in enumerate(pick_head(raw_values_ref.at[part], wide_ref.at[1, part], kv_local)):
            values_ref[lines, pl.ds(k * width, width)] = picked.astype(jnp.bfloat16)


def attend(shards, keys_ref, values_ref, limits_ref, kv_local, steps, own):
    count, width = len(shards), shards[0].shape[1]
    slots = values_ref.shape[0] - lane_width
    scale = width ** (-0.5) * math.log2(math.e)
    queries, step, head = stack(shards, kv_local, steps)
    limit = jnp.concatenate([limits_ref[:, 0:1]] * count, axis=0)
    scores = [
        score(queries, head, keys_ref[:, pl.ds(0, slots)], limit),
        score(queries, head, keys_ref[:, pl.ds(slots, lane_width)], step + 1 if own else step),
    ]
    weights, top, total = weigh(scores, scale)
    begins = (0, slots)
    outputs = None
    for k in range(kv_local):
        columns = pl.ds(k * width, width)
        part = sum(
            jnp.dot(part, values_ref[pl.ds(begin, part.shape[1]), columns], preferred_element_type=jnp.float32)
            for part, begin in zip(weights, begins)
        )
        outputs = part if outputs is None else jnp.where(head == k, part, outputs)
    return outputs, top, total


def own_kernel(kv_local, steps, keys_ref, values_ref, limits_ref, query_ref, outputs_ref, stats_ref):
    outputs, top, total = attend(
        [query_ref[...]], keys_ref, values_ref, limits_ref, kv_local, steps, True
    )
    outputs_ref[...] = outputs
    lane = lax.broadcasted_iota(jnp.int32, stats_ref.shape, 1)
    stats_ref[...] = jnp.where(lane == 0, top, total)


def partner_kernel(kv_local, steps, count, keys_ref, values_ref, limits_ref, *refs):
    shards, packets = refs[-2 * count : -count], refs[-count:]
    rows = shards[0].shape[0]
    results = attend(
        [shard[...] for shard in shards], keys_ref, values_ref, limits_ref, kv_local, steps, False
    )
    for place, packet_ref in enumerate(packets):
        packet_ref[...] = pack(*[part[place * rows : (place + 1) * rows] for part in results])


def merge_parts(rows, outputs_ref, stats_ref, packets):
    stats = stats_ref[...]
    parts = [(outputs_ref[...], stats[:, 0:1], stats[:, 1:2])]
    for packet_ref in packets:
        packet = packet_ref[...].astype(jnp.float32)
        lines = packet[rows : rows + stat_rows]
        parts.append(
            (
                packet[:rows],
                to_column(lines[0:1], rows),
                to_column(lines[1:2] + lines[2:3], rows),
            )
        )
    highest = functools.reduce(jnp.maximum, [top for _, top, _ in parts])
    factors = [jnp.exp2(top - highest) for _, top, _ in parts]
    total = sum(factor * part[2] for factor, part in zip(factors, parts))
    merged = sum(factor * part[0] for factor, part in zip(factors, parts))
    return merged, highest, total


def fold_kernel(rows, outputs_ref, stats_ref, *refs):
    packets, (folded_ref, folded_stats_ref) = refs[:-2], refs[-2:]
    merged, highest, total = merge_parts(rows, outputs_ref, stats_ref, packets)
    folded_ref[...] = merged
    lane = lax.broadcasted_iota(jnp.int32, folded_stats_ref.shape, 1)
    folded_stats_ref[...] = jnp.where(lane == 0, highest, total)


def merge_kernel(rows, outputs_ref, stats_ref, *refs):
    packets, merged_ref = refs[:-1], refs[-1]
    merged, _, total = merge_parts(rows, outputs_ref, stats_ref, packets)
    merged_ref[...] = (merged / total).astype(merged_ref.dtype)


vmem = pl.BlockSpec(memory_space=pltpu.VMEM)
hbm = pl.BlockSpec(memory_space=pltpu.HBM)
grant = 40 * 1024 * 1024


def shift(shard, offset, workers):
    return lax.ppermute(shard, "worker", [(i, (i + offset) % workers) for i in range(workers)])


def local(queries, cache_keys, cache_values, new_keys, new_values, lengths):
    _, steps, heads, width = queries.shape
    slots, kv_local = cache_keys.shape[1:3]
    rows = steps * heads
    workers = lax.axis_size("worker")
    chunks = max(1, slots // 1024)
    flat = lambda cache: cache.reshape(-1, width)
    as_rows = lambda q: q[0].transpose(1, 0, 2).reshape(rows, width)
    packet = jax.ShapeDtypeStruct((rows + stat_rows, width), jnp.bfloat16)

    def prepare():
        return pl.pallas_call(
            functools.partial(prepare_kernel, kv_local, steps, chunks),
            out_shape=(
                jax.ShapeDtypeStruct((kv_local * width, slots + lane_width), jnp.bfloat16),
                jax.ShapeDtypeStruct((slots + lane_width, kv_local * width), jnp.bfloat16),
                jax.ShapeDtypeStruct((rows, lane_width), jnp.int32),
            ),
            in_specs=[hbm] * 5,
            out_specs=(vmem,) * 3,
            scratch_shapes=[
                pltpu.SMEM((1, steps), jnp.int32),
                pltpu.VMEM((slots * kv_local, width), jnp.bfloat16),
                pltpu.VMEM((slots * kv_local, width), jnp.bfloat16),
                pltpu.VMEM((2, steps * kv_local, width), jnp.bfloat16),
                pltpu.VMEM((2, slots * kv_local, width), jnp.float32),
                pltpu.VMEM((2, steps * kv_local, width), jnp.float32),
                pltpu.VMEM((2, lane_width, kv_local * width), jnp.float32),
                pltpu.SemaphoreType.DMA((2, chunks)),
                pltpu.SemaphoreType.DMA((3,)),
            ],
            compiler_params=pltpu.CompilerParams(vmem_limit_bytes=grant),
            name="prepare",
        )(
            *[
                pltpu.with_memory_space_constraint(x, pltpu.HBM)
                for x in (lengths, flat(cache_keys), flat(cache_values), flat(new_keys), flat(new_values))
            ]
        )

    def own(prepared, query_rows):
        return pl.pallas_call(
            functools.partial(own_kernel, kv_local, steps),
            out_shape=(
                jax.ShapeDtypeStruct((rows, width), jnp.float32),
                jax.ShapeDtypeStruct((rows, lane_width), jnp.float32),
            ),
            in_specs=[vmem] * 4,
            out_specs=(vmem,) * 2,
            compiler_params=pltpu.CompilerParams(vmem_limit_bytes=grant),
            name="own_rows",
        )(*prepared, query_rows)

    def partners(prepared, query_list, earlier=()):
        count = len(query_list)
        return pl.pallas_call(
            functools.partial(partner_kernel, kv_local, steps, count),
            out_shape=(packet,) * count,
            in_specs=[vmem] * 3
            + [pl.BlockSpec(memory_space=pl.ANY)] * len(earlier)
            + [vmem] * count,
            out_specs=(vmem,) * count,
            compiler_params=pltpu.CompilerParams(vmem_limit_bytes=grant),
            name="partner_rows",
        )(*prepared, *earlier, *query_list)

    def fold(outputs, stats, packets):
        return pl.pallas_call(
            functools.partial(fold_kernel, rows),
            out_shape=(
                jax.ShapeDtypeStruct((rows, width), jnp.float32),
                jax.ShapeDtypeStruct((rows, lane_width), jnp.float32),
            ),
            in_specs=[vmem] * (2 + len(packets)),
            out_specs=(vmem,) * 2,
            compiler_params=pltpu.CompilerParams(vmem_limit_bytes=grant // 10),
            name="fold",
        )(outputs, stats, *packets)

    def merge(outputs, stats, packets):
        return pl.pallas_call(
            functools.partial(merge_kernel, rows),
            out_shape=jax.ShapeDtypeStruct((rows, width), jnp.bfloat16),
            in_specs=[vmem] * (2 + len(packets)),
            out_specs=vmem,
            compiler_params=pltpu.CompilerParams(vmem_limit_bytes=grant // 10),
            name="merge",
        )(outputs, stats, *packets)

    offsets = list(range(1, workers))
    arrived = {offset: as_rows(shift(queries, offset, workers)) for offset in offsets}
    prepared = prepare()
    sent = {}
    for group, earlier in ((offsets[-1:], offsets[:-1][:1]), (offsets[:-1], [])):
        if group:
            packed = partners(prepared, [arrived[k] for k in group], [arrived[k] for k in earlier])
            sent |= dict(zip(group, packed))
    packets = [shift(sent[workers - offset], offset, workers) for offset in offsets]
    outputs, stats = own(prepared, as_rows(queries))
    stages = [stage for stage in (packets[:1], packets[1:-1], packets[1:][-1:]) if stage]
    for stage in stages[:-1]:
        outputs, stats = fold(outputs, stats, stage)
    merged = merge(outputs, stats, stages[-1] if stages else [])
    return merged.reshape(heads, steps, width).transpose(1, 0, 2)[None]


def solution(mesh):
    split = P(("problem", "worker"), None, "head", None)
    return jax.shard_map(
        local,
        mesh=mesh,
        in_specs=(split,) * 5 + (P(("problem", "worker"), None),),
        out_specs=split,
        check_vma=False,
    )
```
